32 devices in a mesh: parts: 2 (over y), wide: 4 (over z), narrow: 4 (over x, core).
Axes of the slice: x: 2, y: 2, z: 4, core: 2. Of those that a mesh axis runs over, the one named last changes fastest.
Arguments:
- tokens: bfloat16 [2, 256, 7168], P(None, ('parts', 'wide', 'narrow')), parts along dimension 1, may hold values from -6 to 6
- route_copy: int32 [2, 256, 4], P(None, ('parts', 'wide', 'narrow')), parts along dimension 1, may hold values from 0 to 3, as said below
- gate_value: float32 [2, 256, 4], P(None, ('parts', 'wide', 'narrow')), parts along dimension 1, may hold values from 0.05 to 0.6
- w_gate_up: bfloat16 [16, 7168, 512], P(('wide', 'narrow')), may hold values from -0.0625 to 0.0625
- w_down: bfloat16 [16, 256, 7168], P(('wide', 'narrow')), may hold values from -0.1875 to 0.1875
Outputs:
- mixed: bfloat16 [2, 256, 7168], P(None, ('parts', 'wide', 'narrow')), parts along dimension 1
The draws below stay inside these ranges and needn't reach their ends.
There are 2 independent parts, one for each index of `parts`. The reference program is written for one: setup_inputs(seed, part) draws one part's arguments, and reference() takes and returns one part's arrays. A program takes and returns all parts, laid end to end along the dimension named above; an argument that names none is the same for every part. Nothing has to cross between parts.
Inputs may be any that keep to these rules, and one draw needn't show every extreme that they name: `route_copy`: each token names 4 different copies; copy c belongs to node group c, and one token's copies lie in at most 4 node groups. Within one step the 8 tokens of one device (aligned blocks of rows) name no copy more than 8 times.
All inputs are finite; a program needn't handle non-finite values.
Results may differ from the reference program's by a relative error of at most 0.013.
Values may be sent and summed in bfloat16 or wider, within the bound.
A program may use at most 128 MiB of HBM per device.

```python
import math
import jax
import jax.numpy as jnp
from jax import lax

D = 7168
HW = 1024
SPLIT = 4
STEPS = 2
TOK_DEV = 8
HW_DEV = 256
COPIES = 4
GROUP_COPIES = 1
TOPK = 4
NODE_LIMIT = 4
CAP = 8
TOKENS = 128
N_WIDE = 4
N_NARROW = 4


def draw_route_copy(key, part):
    key = jax.random.fold_in(key, 11)
    block_count = STEPS * TOKENS // TOK_DEV
    key_pop, key_hot, key_block, key_noise, key_perm = jax.random.split(key, 5)
    popular = jax.random.randint(key_pop, (COPIES,), 0, 4)
    hot_all = jax.random.randint(key_hot, (), 0, COPIES)
    hot_block = jax.random.randint(key_block, (block_count,), 0, COPIES)
    noise = jax.random.randint(key_noise, (block_count, TOK_DEV, COPIES), 0, 1024)
    copy_ids = jnp.arange(COPIES, dtype=jnp.int32)
    value = noise + popular[None, None, :] * 512
    value = value + jnp.where(copy_ids[None, None, :] == hot_all, 16384, 0)
    value = value + jnp.where(copy_ids[None, None, :] == hot_block[:, None, None], 8192, 0)
    scores = (value * COPIES + copy_ids[None, None, :]).astype(jnp.int32)
    group_ids = jnp.arange(N_WIDE, dtype=jnp.int32)

    def choose(counts, score_row):
        free = counts < CAP
        score = jnp.where(free, score_row, -1)
        avail = jnp.sum(free.reshape(N_WIDE, GROUP_COPIES).astype(jnp.int32), axis=1)
        best = jnp.max(score.reshape(N_WIDE, GROUP_COPIES), axis=1)
        group_key = avail * 16777216 + best
        _, groups = lax.top_k(group_key, NODE_LIMIT)
        chosen = jnp.any(group_ids[:, None] == groups[None, :], axis=1)
        in_group = jnp.repeat(chosen, GROUP_COPIES)
        final = jnp.where(in_group, score, -2)
        _, picks = lax.top_k(final, TOPK)
        picks = picks.astype(jnp.int32)
        added = jnp.sum((picks[:, None] == copy_ids[None, :]).astype(jnp.int32), axis=0)
        return (counts + added, picks)

    def one_block(block_scores, block_key):
        _, picks = lax.scan(choose, jnp.zeros((COPIES,), jnp.int32), block_scores)
        order = jax.random.permutation(block_key, TOK_DEV)
        return picks[order]
    block_keys = jax.random.split(key_perm, block_count)
    routes = jax.vmap(one_block)(scores, block_keys)
    return routes.reshape(STEPS, TOKENS, TOPK).astype(jnp.int32)


def block_scale(key, extent, shards, low, high):
    level, own = 1.0, jax.random.fold_in(key, 6)
    for axis_at, parts in shards:
        draws = jnp.exp(jax.random.uniform(jax.random.fold_in(own, axis_at), (parts,), jnp.float32, low / len(shards), high / len(shards)))
        level = level * jnp.repeat(draws, extent[axis_at] // parts).reshape([-1 if axis == axis_at else 1 for axis in range(len(extent))])
    return level


def gaussian(key, extent, spread, limit, shards=(), kind=jnp.bfloat16):
    gain = block_scale(key, extent, shards, -0.22, 0.18) if shards else 1.0
    array = jax.random.normal(key, extent, jnp.float32) * spread * gain
    return jnp.minimum(jnp.maximum(array, -limit), limit).astype(kind)


def setup_inputs(seed: int = 0, part: int = 0) -> dict:
    arg_keys = jax.random.split(jax.random.key(seed), 6)
    own_keys = jax.random.split(jax.random.fold_in(arg_keys[5], part), 6)
    return {
        "tokens": gaussian(own_keys[0], (STEPS, TOKENS, D), 1.0, 6.0, ((1, 16),)),
        "route_copy": draw_route_copy(jax.random.fold_in(jax.random.fold_in(arg_keys[5], part), 71), part),
        "gate_value": jnp.clip(jnp.exp(math.log(0.6) - 2.4849067 * jax.random.uniform(own_keys[2], (STEPS, TOKENS, TOPK), jnp.float32) ** block_scale(own_keys[2], (STEPS, TOKENS, TOPK), ((1, 16),), -0.2, 0.2)), 0.05, 0.6),
        "w_gate_up": gaussian(arg_keys[3], (COPIES * SPLIT, D, 2 * HW_DEV), D ** -0.5, 0.0625, ((0, 16),)),
        "w_down": gaussian(arg_keys[4], (COPIES * SPLIT, HW_DEV, D), HW ** -0.5, 0.1875, ((0, 16),)),
    }


def expert_block(row_block, gate_up, down, width):
    joined = jnp.dot(row_block, gate_up, preferred_element_type=jnp.float32)
    hidden = (jax.nn.silu(joined[:, :width]) * joined[:, width:]).astype(jnp.bfloat16)
    return jnp.dot(hidden, down, preferred_element_type=jnp.float32).astype(jnp.bfloat16)


def reference(tokens, route_copy, gate_value, w_gate_up, w_down):
    dev_count = N_WIDE * N_NARROW
    slot_total = dev_count * CAP
    results = []
    for step_index in range(STEPS):
        route_now = route_copy[step_index].reshape(dev_count, TOK_DEV, TOPK)
        one_hot = (route_now[..., None] == jnp.arange(COPIES, dtype=jnp.int32)).astype(jnp.int32)
        counts = jnp.sum(one_hot, axis=2)
        before = jnp.cumsum(counts, axis=1) - counts
        ranked = jnp.sum(one_hot * before[:, :, None, :], axis=-1).astype(jnp.int32)
        device_ids = jnp.arange(dev_count, dtype=jnp.int32)[:, None, None]
        target = (route_now * slot_total + device_ids * CAP + ranked).reshape(-1)
        token_ids = jnp.broadcast_to(jnp.arange(TOKENS, dtype=jnp.int32).reshape(dev_count, TOK_DEV, 1), route_now.shape).reshape(-1)
        owner = jnp.full((COPIES * slot_total,), TOKENS, jnp.int32).at[target].set(token_ids).reshape(COPIES, slot_total)
        gains = jnp.zeros((COPIES * slot_total,), jnp.float32).at[target].set(gate_value[step_index].reshape(-1)).reshape(COPIES, slot_total)
        owner = jnp.repeat(owner, SPLIT, axis=0)
        gains = jnp.repeat(gains, SPLIT, axis=0)
        padded = jnp.concatenate([tokens[step_index], jnp.zeros((1, D), jnp.bfloat16)], axis=0)

        def visit(total, packet):
            owners, gain_row, gate_up, down = packet
            produced = expert_block(padded[owners], gate_up, down, HW_DEV)
            total = total.at[owners].add(gain_row[:, None] * produced.astype(jnp.float32), mode="drop")
            return total, None

        total, _ = lax.scan(visit, jnp.zeros((TOKENS, D), jnp.float32), (owner, gains, w_gate_up, w_down))
        results.append(total.astype(jnp.bfloat16))
    return jnp.stack(results)
```

```python
import functools

import jax
import jax.numpy as jnp
from jax import lax
from jax.experimental import pallas as pl
from jax.experimental.pallas import tpu as pltpu
from jax.sharding import PartitionSpec as P

SPLIT = 4


def from_partner(block, axis, bit):
    count = lax.axis_size(axis)
    route = []
    for low in range(count):
        high = low | 1 << bit
        if high != low and high < count:
            route += [(low, high), (high, low)]
    return lax.ppermute(block, axis, route)


def expert_block(packet, gate_up, down):
    width = down.shape[0]
    lead = packet.shape[:-1]
    row_block = packet.reshape(-1, packet.shape[-1])
    joined = jnp.dot(row_block, gate_up, preferred_element_type=jnp.float32)
    hidden = (jax.nn.silu(joined[:, :width]) * joined[:, width:]).astype(jnp.bfloat16)
    produced = jnp.dot(hidden, down, preferred_element_type=jnp.float32).astype(jnp.bfloat16)
    return produced.reshape(lead + (down.shape[1],))


def rank_pairs(route_now, copy_count):
    one_hot = (route_now[..., None] == jnp.arange(copy_count, dtype=jnp.int32)).astype(jnp.int32)
    counts = jnp.sum(one_hot, axis=-2)
    before = jnp.cumsum(counts, axis=-2) - counts
    return jnp.sum(one_hot * before[..., None, :], axis=-1)


def select_rows(target, gates, slot_total):
    matches = target[None, :, :] == jnp.arange(slot_total, dtype=jnp.int32)[:, None, None]
    picker = jnp.any(matches, axis=-1).astype(jnp.bfloat16)
    weights = jnp.sum(jnp.where(matches, gates[None, :, :], 0.0), axis=-1)
    return (picker, weights)


def body(tokens, route_copy, gate_value, w_gate_up, w_down):
    num_steps, tok_rows, model_dim = tokens.shape
    top_count = route_copy.shape[2]
    wide_count = lax.axis_size("wide")
    narrow_count = lax.axis_size("narrow")
    dev_count = wide_count * narrow_count
    copy_count = dev_count // SPLIT
    slot_cap = min(tok_rows, max(2, 3 * tok_rows * top_count // (2 * copy_count) + tok_rows // 64))
    gate_up = w_gate_up[0]
    down = w_down[0]
    results = []
    for step_index in range(num_steps):
        step_rows = tokens[step_index]
        step_route = route_copy[step_index]
        step_gate = gate_value[step_index]
        piece_rows = (slot_cap + SPLIT - 1) // SPLIT
        per_copy = SPLIT * piece_rows
        ranked = rank_pairs(step_route, copy_count)
        target = step_route * per_copy + ranked
        picker, weights = select_rows(target, step_gate, copy_count * per_copy)
        outbox = jnp.dot(picker, step_rows, preferred_element_type=jnp.float32).astype(jnp.bfloat16)
        outbox = outbox.reshape(dev_count, piece_rows, model_dim)
        received = lax.all_to_all(
            outbox, ("wide", "narrow"), split_axis=0, concat_axis=0, tiled=True
        )
        narrow_index = lax.axis_index("narrow")
        shared = received
        for bit_number in range(SPLIT.bit_length() - 1):
            other = from_partner(shared, "narrow", bit_number)
            upper = narrow_index >> bit_number & 1 == 1
            shared = jnp.where(
                upper,
                jnp.concatenate([other, shared], axis=1),
                jnp.concatenate([shared, other], axis=1),
            )
        produced = expert_block(shared[:, :slot_cap], gate_up, down)
        returned = lax.all_to_all(
            produced, ("wide", "narrow"), split_axis=0, concat_axis=0, tiled=True
        )
        summed = jnp.sum(
            returned.reshape(copy_count, SPLIT, slot_cap, model_dim).astype(jnp.float32), axis=1
        )
        used = weights.reshape(copy_count, per_copy, tok_rows)[:, :slot_cap].reshape(
            copy_count * slot_cap, tok_rows
        )
        total = jnp.dot(
            used.T,
            summed.reshape(copy_count * slot_cap, model_dim),
            precision=lax.Precision.HIGHEST,
        )
        results.append(total.astype(jnp.bfloat16))
    return jnp.stack(results)


NUM_CHUNKS = 4
LANES = 128
THIRD = 32
MESH = pl.DeviceIdType.MESH


def dense_kernel(
    wide_count, tok_ref, route_ref, gate_ref, up_hbm, down_hbm, out_ref,
    held, up, down, acc, hid, core_out, core_in, core_own, x_out, x_in, x_own, z_out, z_in,
    up_sem, down_sem, gz_s, gz_r, gx_s, gx_r, ga_s, ga_r, gb_s, gb_r,
    rc_s, rc_r, rx_s, rx_r, rz_s, rz_r,
):
    rows, dim = tok_ref.shape
    width = down.shape[0]
    size = dim // NUM_CHUNKS
    part = lax.axis_index("parts")
    z = lax.axis_index("wide")
    narrow = lax.axis_index("narrow")
    x = narrow // 2
    c = narrow % 2
    x_peer = (part, z, (1 - x) * 2 + c)
    c_peer = (part, z, x * 2 + 1 - c)
    offsets = list(range(1, wide_count))
    z_peers = {k: lax.rem(z + k, wide_count) for k in offsets}
    z_from = {k: lax.rem(z + wide_count - k, wide_count) for k in offsets}
    z_from[0] = z

    def block(index):
        return pl.ds(pl.multiple_of(index * rows, rows), rows)

    def held_cols(ch):
        if ch == 0:
            return pl.ds(0, LANES + size)
        return pl.ds(LANES + ch * size, size)

    up_copies = []
    for ch in range(NUM_CHUNKS):
        span = pl.ds(ch * size, size)
        copy = pltpu.make_async_copy(up_hbm.at[span], up.at[span], up_sem.at[ch])
        copy.start()
        up_copies.append(copy)
    down_copy = pltpu.make_async_copy(down_hbm, down, down_sem)
    down_copy.start()

    barrier = pltpu.get_barrier_semaphore()
    peers = [(part, z_peers[k], narrow) for k in offsets] + [x_peer, c_peer]
    for peer in peers:
        pl.semaphore_signal(barrier, inc=1, device_id=peer, device_id_type=MESH)

    lane = lax.broadcasted_iota(jnp.int32, (rows, LANES), 1)
    weight = jnp.zeros((rows, LANES), jnp.float32)
    for k in range(route_ref.shape[1]):
        weight += jnp.where(lane % THIRD == route_ref[:, k : k + 1], gate_ref[:, k : k + 1], 0.0)
    high = weight.astype(jnp.bfloat16).astype(jnp.float32)
    mid = (weight - high).astype(jnp.bfloat16).astype(jnp.float32)
    low = weight - high - mid
    coded = jnp.where(
        lane < THIRD, high, jnp.where(lane < 2 * THIRD, mid, jnp.where(lane < 3 * THIRD, low, 0.0))
    )
    held[x, c, block(z), 0:LANES] = coded.astype(jnp.bfloat16)
    held[x, c, block(z), LANES:] = tok_ref[...]

    pl.semaphore_wait(barrier, len(peers))

    sends = []

    def remote(src, dst, send_sem, recv_sem, peer):
        copy = pltpu.make_async_remote_copy(
            src_ref=src, dst_ref=dst, send_sem=send_sem, recv_sem=recv_sem,
            device_id=peer, device_id_type=MESH,
        )
        sends.append(copy)
        return copy

    z_copy, x_copy, a_copy, b_copy = {}, {}, {}, {}
    for ch in range(NUM_CHUNKS):
        own = held.at[x, c, block(z), held_cols(ch)]
        for k in offsets:
            z_copy[ch, k] = remote(
                own, own, gz_s.at[ch, k], gz_r.at[ch, k], (part, z_peers[k], narrow)
            )
            z_copy[ch, k].start()
        x_copy[ch, 0] = remote(own, own, gx_s.at[ch, 0], gx_r.at[ch, 0], x_peer)
        x_copy[ch, 0].start()

    def gather_a(ch):
        for k in offsets:
            z_copy[ch, k].wait_recv()
            ref = held.at[x, c, block(z_from[k]), held_cols(ch)]
            x_copy[ch, k] = remote(ref, ref, gx_s.at[ch, k], gx_r.at[ch, k], x_peer)
            x_copy[ch, k].start()
        ref = held.at[x, c, :, held_cols(ch)]
        a_copy[ch] = remote(ref, ref, ga_s.at[ch], ga_r.at[ch], c_peer)
        a_copy[ch].start()

    def gather_b(ch):
        for k in [0] + offsets:
            x_copy[ch, k].wait_recv()
        ref = held.at[1 - x, c, :, held_cols(ch)]
        b_copy[ch] = remote(ref, ref, gb_s.at[ch], gb_r.at[ch], c_peer)
        b_copy[ch].start()

    def gather_c(ch):
        a_copy[ch].wait_recv()
        b_copy[ch].wait_recv()
        up_copies[ch].wait()
        cols = held[:, :, :, LANES + ch * size : LANES + (ch + 1) * size]
        term = jnp.dot(
            cols.reshape(-1, size), up[ch * size : (ch + 1) * size, :],
            preferred_element_type=jnp.float32,
        )
        if ch == 0:
            acc[...] = term
        else:
            acc[...] += term

    for i in range(NUM_CHUNKS + 2):
        if i < NUM_CHUNKS:
            gather_a(i)
        if 0 <= i - 1 < NUM_CHUNKS:
            gather_b(i - 1)
        if 0 <= i - 2:
            gather_c(i - 2)

    joined = acc[...]
    gate = joined[:, :width]
    value = gate / (1.0 + jnp.exp(-gate)) * joined[:, width:]
    hid[...] = value.astype(jnp.bfloat16).reshape(hid.shape)
    down_copy.wait()

    def row_weights(core):
        coded = held[:, core, :, 0:LANES].reshape(-1, LANES).astype(jnp.float32)
        lane = lax.broadcasted_iota(jnp.int32, coded.shape, 1)
        return jnp.sum(jnp.where(lane % THIRD == z, coded, 0.0), axis=1, keepdims=True)

    other_weight = row_weights(1 - c)
    own_weight = row_weights(c)
    half = (2, wide_count * rows, size)
    rc, rx, rz = {}, {}, {}

    def scatter_a(ch):
        cols = slice(ch * size, (ch + 1) * size)
        out = jnp.dot(
            hid[:, 1 - c].reshape(-1, width), down[:, cols], preferred_element_type=jnp.float32
        )
        core_out[ch] = (out * other_weight).astype(jnp.bfloat16).reshape(half)
        rc[ch] = remote(core_out.at[ch], core_in.at[ch], rc_s.at[ch], rc_r.at[ch], c_peer)
        rc[ch].start()
        out = jnp.dot(
            hid[:, c].reshape(-1, width), down[:, cols], preferred_element_type=jnp.float32
        )
        core_own[ch] = (out * own_weight).reshape(half)

    def scatter_b(ch):
        rc[ch].wait_recv()
        out = core_own[ch, 1 - x] + core_in[ch, 1 - x].astype(jnp.float32)
        x_out[ch] = out.astype(jnp.bfloat16)
        rx[ch] = remote(x_out.at[ch], x_in.at[ch], rx_s.at[ch], rx_r.at[ch], x_peer)
        rx[ch].start()
        x_own[ch] = core_own[ch, x] + core_in[ch, x].astype(jnp.float32)

    def scatter_c(ch):
        rx[ch].wait_recv()
        out = x_own[ch] + x_in[ch].astype(jnp.float32)
        x_own[ch] = out
        z_out[ch] = out.astype(jnp.bfloat16)
        for k in offsets:
            rz[ch, k] = remote(
                z_out.at[ch, block(z_peers[k])], z_in.at[ch, k - 1],
                rz_s.at[ch, k], rz_r.at[ch, k], (part, z_peers[k], narrow),
            )
            rz[ch, k].start()

    def scatter_d(ch):
        out = x_own[ch, block(z), :]
        for k in offsets:
            rz[ch, k].wait_recv()
            out += z_in[ch, k - 1].astype(jnp.float32)
        out_ref[:, ch * size : (ch + 1) * size] = out.astype(jnp.bfloat16)

    for i in range(NUM_CHUNKS + 1):
        if i < NUM_CHUNKS:
            scatter_a(i)
        if 0 <= i - 1:
            scatter_b(i - 1)
    for i in range(NUM_CHUNKS + 1):
        if i < NUM_CHUNKS:
            scatter_c(i)
        if 0 <= i - 1:
            scatter_d(i - 1)
    for copy in sends:
        copy.wait_send()


def dense_body(tokens, route_copy, gate_value, w_gate_up, w_down):
    num_steps, tok_rows, dim = tokens.shape
    rows = num_steps * tok_rows
    wide_count = lax.axis_size("wide")
    width = w_down.shape[1]
    size = dim // NUM_CHUNKS
    col = wide_count * rows
    bf16, f32 = jnp.bfloat16, jnp.float32
    vmem = pl.BlockSpec(memory_space=pltpu.VMEM)
    hbm = pl.BlockSpec(memory_space=pl.ANY)
    dma = pltpu.SemaphoreType.DMA
    n = NUM_CHUNKS
    out = pl.pallas_call(
        functools.partial(dense_kernel, wide_count),
        out_shape=jax.ShapeDtypeStruct((rows, dim), bf16),
        in_specs=[vmem, vmem, vmem, hbm, hbm],
        out_specs=vmem,
        scratch_shapes=[
            pltpu.VMEM((2, 2, col, LANES + dim), bf16),
            pltpu.VMEM((dim, 2 * width), bf16),
            pltpu.VMEM((width, dim), bf16),
            pltpu.VMEM((4 * col, 2 * width), f32),
            pltpu.VMEM((2, 2, col, width), bf16),
            pltpu.VMEM((n, 2, col, size), bf16),
            pltpu.VMEM((n, 2, col, size), bf16),
            pltpu.VMEM((n, 2, col, size), f32),
            pltpu.VMEM((n, col, size), bf16),
            pltpu.VMEM((n, col, size), bf16),
            pltpu.VMEM((n, col, size), f32),
            pltpu.VMEM((n, col, size), bf16),
            pltpu.VMEM((n, wide_count - 1, rows, size), bf16),
            dma((n,)), dma,
            dma((n, wide_count)), dma((n, wide_count)),
            dma((n, wide_count)), dma((n, wide_count)),
            dma((n,)), dma((n,)), dma((n,)), dma((n,)),
            dma((n,)), dma((n,)), dma((n,)), dma((n,)),
            dma((n, wide_count)), dma((n, wide_count)),
        ],
        compiler_params=pltpu.CompilerParams(
            collective_id=0, has_side_effects=True, vmem_limit_bytes=56 * 1024 * 1024
        ),
        cost_estimate=pl.CostEstimate(
            flops=12 * col * dim * width * 2, bytes_accessed=3 * dim * width * 2, transcendentals=0
        ),
    )(
        tokens.reshape(rows, dim),
        route_copy.reshape(rows, -1),
        gate_value.reshape(rows, -1),
        w_gate_up[0],
        w_down[0],
    )
    return out.reshape(num_steps, tok_rows, dim)


def choose_body(tokens, route_copy, gate_value, w_gate_up, w_down):
    wide_count = lax.axis_size("wide")
    narrow_count = lax.axis_size("narrow")
    copy_count = wide_count * narrow_count // SPLIT
    every_copy = route_copy.shape[2] == copy_count and copy_count <= THIRD
    whole_rows = tokens.shape[0] * tokens.shape[1] % 16 == 0
    if every_copy and whole_rows and narrow_count == SPLIT:
        return dense_body(tokens, route_copy, gate_value, w_gate_up, w_down)
    return body(tokens, route_copy, gate_value, w_gate_up, w_down)


def solution(mesh):
    return jax.shard_map(
        choose_body,
        mesh=mesh,
        in_specs=(
            P(None, ("parts", "wide", "narrow"), None),
            P(None, ("parts", "wide", "narrow"), None),
            P(None, ("parts", "wide", "narrow"), None),
            P(("wide", "narrow"), None, None),
            P(("wide", "narrow"), None, None),
        ),
        out_specs=P(None, ("parts", "wide", "narrow"), None),
        check_vma=False,
    )
```

```python
import functools

import jax
import jax.numpy as jnp
from jax import lax
from jax.experimental import pallas as pl
from jax.experimental.pallas import tpu as pltpu
from jax.sharding import PartitionSpec as P

SPLIT = 4


def from_partner(block, axis, bit):
    count = lax.axis_size(axis)
    route = []
    for low in range(count):
        high = low | 1 << bit
        if high != low and high < count:
            route += [(low, high), (high, low)]
    return lax.ppermute(block, axis, route)


def expert_block(packet, gate_up, down):
    width = down.shape[0]
    lead = packet.shape[:-1]
    row_block = packet.reshape(-1, packet.shape[-1])
    joined = jnp.dot(row_block, gate_up, preferred_element_type=jnp.float32)
    hidden = (jax.nn.silu(joined[:, :width]) * joined[:, width:]).astype(jnp.bfloat16)
    produced = jnp.dot(hidden, down, preferred_element_type=jnp.float32).astype(jnp.bfloat16)
    return produced.reshape(lead + (down.shape[1],))


def rank_pairs(route_now, copy_count):
    one_hot = (route_now[..., None] == jnp.arange(copy_count, dtype=jnp.int32)).astype(jnp.int32)
    counts = jnp.sum(one_hot, axis=-2)
    before = jnp.cumsum(counts, axis=-2) - counts
    return jnp.sum(one_hot * before[..., None, :], axis=-1)


def select_rows(target, gates, slot_total):
    matches = target[None, :, :] == jnp.arange(slot_total, dtype=jnp.int32)[:, None, None]
    picker = jnp.any(matches, axis=-1).astype(jnp.bfloat16)
    weights = jnp.sum(jnp.where(matches, gates[None, :, :], 0.0), axis=-1)
    return (picker, weights)


def body(tokens, route_copy, gate_value, w_gate_up, w_down):
    num_steps, tok_rows, model_dim = tokens.shape
    top_count = route_copy.shape[2]
    wide_count = lax.axis_size("wide")
    narrow_count = lax.axis_size("narrow")
    dev_count = wide_count * narrow_count
    copy_count = dev_count // SPLIT
    slot_cap = min(tok_rows, max(2, 3 * tok_rows * top_count // (2 * copy_count) + tok_rows // 64))
    gate_up = w_gate_up[0]
    down = w_down[0]
    results = []
    for step_index in range(num_steps):
        step_rows = tokens[step_index]
        step_route = route_copy[step_index]
        step_gate = gate_value[step_index]
        piece_rows = (slot_cap + SPLIT - 1) // SPLIT
        per_copy = SPLIT * piece_rows
        ranked = rank_pairs(step_route, copy_count)
        target = step_route * per_copy + ranked
        picker, weights = select_rows(target, step_gate, copy_count * per_copy)
        outbox = jnp.dot(picker, step_rows, preferred_element_type=jnp.float32).astype(jnp.bfloat16)
        outbox = outbox.reshape(dev_count, piece_rows, model_dim)
        received = lax.all_to_all(
            outbox, ("wide", "narrow"), split_axis=0, concat_axis=0, tiled=True
        )
        narrow_index = lax.axis_index("narrow")
        shared = received
        for bit_number in range(SPLIT.bit_length() - 1):
            other = from_partner(shared, "narrow", bit_number)
            upper = narrow_index >> bit_number & 1 == 1
            shared = jnp.where(
                upper,
                jnp.concatenate([other, shared], axis=1),
                jnp.concatenate([shared, other], axis=1),
            )
        produced = expert_block(shared[:, :slot_cap], gate_up, down)
        returned = lax.all_to_all(
            produced, ("wide", "narrow"), split_axis=0, concat_axis=0, tiled=True
        )
        summed = jnp.sum(
            returned.reshape(copy_count, SPLIT, slot_cap, model_dim).astype(jnp.float32), axis=1
        )
        used = weights.reshape(copy_count, per_copy, tok_rows)[:, :slot_cap].reshape(
            copy_count * slot_cap, tok_rows
        )
        total = jnp.dot(
            used.T,
            summed.reshape(copy_count * slot_cap, model_dim),
            precision=lax.Precision.HIGHEST,
        )
        results.append(total.astype(jnp.bfloat16))
    return jnp.stack(results)


NUM_CHUNKS = 4
CROSS_FIRST = (3,)
LANES = 128
THIRD = 32
MESH = pl.DeviceIdType.MESH


def dense_kernel(
    wide_count, tok_ref, route_ref, gate_ref, up_hbm, down_hbm, out_ref,
    held, up, down, acc, hid, core_out, core_in, core_own, x_out, x_in, x_own, z_out, z_in,
    last_out, last_in,
    up_sem, down_sem, gz_s, gz_r, gx_s, gx_r, ga_s, ga_r, gb_s, gb_r,
    rc_s, rc_r, rx_s, rx_r, rz_s, rz_r,
):
    rows, dim = tok_ref.shape
    num_steps, top_count, tok_rows = route_ref.shape
    width = down.shape[0]
    size = dim // NUM_CHUNKS
    part = lax.axis_index("parts")
    z = lax.axis_index("wide")
    narrow = lax.axis_index("narrow")
    x = narrow // 2
    c = narrow % 2
    x_peer = (part, z, (1 - x) * 2 + c)
    c_peer = (part, z, x * 2 + 1 - c)
    end = wide_count - 1
    has_low, has_high = z > 0, z < end
    signs = (1, -1)
    steps = [(h, s) for h in range(end) for s in range(2)]

    def block(index):
        return pl.ds(pl.multiple_of(index * rows, rows), rows)

    def cols_of(ch):
        if ch == 0:
            return pl.ds(0, LANES + size)
        return pl.ds(LANES + ch * size, size)

    def z_peer(s):
        return (part, z + signs[s], narrow)

    up_copies = []
    for ch in range(NUM_CHUNKS):
        span = pl.ds(ch * size, size)
        copy = pltpu.make_async_copy(up_hbm.at[span], up.at[span], up_sem.at[ch])
        copy.start()
        up_copies.append(copy)
    down_copy = pltpu.make_async_copy(down_hbm, down, down_sem)
    down_copy.start()

    barrier = pltpu.get_barrier_semaphore()

    def greet(peer):
        pl.semaphore_signal(barrier, inc=1, device_id=peer, device_id_type=MESH)

    pl.when(has_high)(lambda: greet(z_peer(0)))
    pl.when(has_low)(lambda: greet(z_peer(1)))
    greet(x_peer)
    greet(c_peer)

    eye = lax.broadcasted_iota(jnp.int32, (tok_rows, tok_rows), 0) == lax.broadcasted_iota(
        jnp.int32, (tok_rows, tok_rows), 1
    )
    lane = lax.broadcasted_iota(jnp.int32, (tok_rows, LANES), 1)
    coded_steps = []
    for step in range(num_steps):
        weight = jnp.zeros((tok_rows, LANES), jnp.float32)
        for k in range(top_count):
            route = jnp.where(eye, route_ref[step, k : k + 1, :], 0)
            route = jnp.sum(route, axis=1, keepdims=True)
            gate = jnp.where(eye, gate_ref[step, k : k + 1, :], 0.0)
            gate = jnp.sum(gate, axis=1, keepdims=True)
            weight += jnp.where(lane % THIRD == route, gate, 0.0)
        high = weight.astype(jnp.bfloat16).astype(jnp.float32)
        mid = (weight - high).astype(jnp.bfloat16).astype(jnp.float32)
        low = weight - high - mid
        low = jnp.where(lane < 3 * THIRD, low, 0.0)
        coded_steps.append(jnp.where(lane < THIRD, high, jnp.where(lane < 2 * THIRD, mid, low)))
    coded = jnp.concatenate(coded_steps, axis=0).astype(jnp.bfloat16)
    held[x, c, block(z), 0:LANES] = coded
    held[x, c, block(z), LANES:] = tok_ref[...]

    pl.semaphore_wait(barrier, 2 + has_low.astype(jnp.int32) + has_high.astype(jnp.int32))

    sends = []

    def remote(src, dst, send_sem, recv_sem, peer):
        return pltpu.make_async_remote_copy(
            src_ref=src, dst_ref=dst, send_sem=send_sem, recv_sem=recv_sem,
            device_id=peer, device_id_type=MESH,
        )

    def launch(make, *cond):
        def go():
            make().start()

        def finish():
            make().wait_send()

        if cond:
            pl.when(cond[0])(go)
            sends.append(lambda: pl.when(cond[0])(finish))
        else:
            go()
            sends.append(finish)

    def can_recv(h, s):
        return z >= h + 1 if s == 0 else z + h + 1 <= end

    def can_send(h, s):
        return (z >= h) & has_high if s == 0 else (z + h <= end) & has_low

    def z_ref(ch, index):
        if ch in CROSS_FIRST:
            return held.at[:, c, block(index), cols_of(ch)]
        return held.at[x, c, block(index), cols_of(ch)]

    def stream(ch, h, s):
        ref = z_ref(ch, z - signs[s] * h)
        return remote(ref, ref, gz_s.at[ch, s, h], gz_r.at[ch, s, h], z_peer(s))

    def arrival(ch, h, s):
        ref = z_ref(ch, z - signs[s] * (h + 1))
        return remote(ref, ref, gz_s.at[ch, s, h], gz_r.at[ch, s, h], x_peer)

    def own_x(ch):
        ref = held.at[x, c, block(z), cols_of(ch)]
        return remote(ref, ref, gx_s.at[ch, 2, 0], gx_r.at[ch, 2, 0], x_peer)

    def forward_x(ch, h, s):
        ref = held.at[x, c, block(z - signs[s] * (h + 1)), cols_of(ch)]
        return remote(ref, ref, gx_s.at[ch, s, h], gx_r.at[ch, s, h], x_peer)

    def core_a(ch):
        if ch in CROSS_FIRST:
            ref = held.at[:, c, :, cols_of(ch)]
        else:
            ref = held.at[x, c, :, cols_of(ch)]
        return remote(ref, ref, ga_s.at[ch], ga_r.at[ch], c_peer)

    def core_b(ch):
        ref = held.at[1 - x, c, :, cols_of(ch)]
        return remote(ref, ref, gb_s.at[ch], gb_r.at[ch], c_peer)

    for ch in range(NUM_CHUNKS):
        if ch not in CROSS_FIRST:
            for s in range(2):
                launch(functools.partial(stream, ch, 0, s), can_send(0, s))
        launch(functools.partial(own_x, ch))

    def gather_first(ch):
        if ch in CROSS_FIRST:
            own_x(ch).wait_recv()
            for s in range(2):
                launch(functools.partial(stream, ch, 0, s), can_send(0, s))

    def gather_a(ch, h):
        for s in range(2):
            pl.when(can_recv(h, s))(lambda h=h, s=s: arrival(ch, h, s).wait_recv())
            if h + 1 < end:
                launch(functools.partial(stream, ch, h + 1, s), can_send(h + 1, s))
            if ch not in CROSS_FIRST:
                launch(functools.partial(forward_x, ch, h, s), can_recv(h, s))
        if h + 1 == end:
            launch(functools.partial(core_a, ch))

    def gather_b(ch):
        if ch not in CROSS_FIRST:
            own_x(ch).wait_recv()
            for h, s in steps:
                pl.when(can_recv(h, s))(lambda h=h, s=s: forward_x(ch, h, s).wait_recv())
            launch(functools.partial(core_b, ch))

    def gather_c(ch):
        core_a(ch).wait_recv()
        if ch not in CROSS_FIRST:
            core_b(ch).wait_recv()
        up_copies[ch].wait()
        cols = held[:, :, :, LANES + ch * size : LANES + (ch + 1) * size]
        term = jnp.dot(
            cols.reshape(-1, size), up[ch * size : (ch + 1) * size, :],
            preferred_element_type=jnp.float32,
        )
        if ch == 0:
            acc[...] = term
        else:
            acc[...] += term

    for i in range(NUM_CHUNKS + end + 1):
        if i < NUM_CHUNKS:
            gather_first(i)
        for h in range(end):
            if 0 <= i - h < NUM_CHUNKS:
                gather_a(i - h, h)
        if 0 <= i - end < NUM_CHUNKS:
            gather_b(i - end)
        if 0 <= i - end - 1:
            gather_c(i - end - 1)

    joined = acc[...]
    gate = joined[:, :width]
    value = gate / (1.0 + jnp.exp(-gate)) * joined[:, width:]
    hid[...] = value.astype(jnp.bfloat16).reshape(hid.shape)
    down_copy.wait()

    def row_weights(core):
        coded = held[:, core, :, 0:LANES].reshape(-1, LANES).astype(jnp.float32)
        lane = lax.broadcasted_iota(jnp.int32, coded.shape, 1)
        return jnp.sum(jnp.where(lane % THIRD == z, coded, 0.0), axis=1, keepdims=True)

    other_weight = row_weights(1 - c)
    own_weight = row_weights(c)
    half = (2, wide_count * rows, size)

    def rc(ch):
        return remote(core_out.at[ch], core_in.at[ch], rc_s.at[ch], rc_r.at[ch], c_peer)

    def rx(ch):
        if ch in CROSS_FIRST:
            at = CROSS_FIRST.index(ch)
            return remote(last_out.at[at], last_in.at[at], rx_s.at[ch], rx_r.at[ch], x_peer)
        return remote(x_out.at[ch], x_in.at[ch], rx_s.at[ch], rx_r.at[ch], x_peer)

    def scatter_a(ch):
        cols = slice(ch * size, (ch + 1) * size)
        out = jnp.dot(
            hid[:, 1 - c].reshape(-1, width), down[:, cols], preferred_element_type=jnp.float32
        )
        core_out[ch] = (out * other_weight).astype(jnp.bfloat16).reshape(half)
        launch(functools.partial(rc, ch))
        out = jnp.dot(
            hid[:, c].reshape(-1, width), down[:, cols], preferred_element_type=jnp.float32
        )
        core_own[ch] = (out * own_weight).reshape(half)

    def scatter_b(ch):
        rc(ch).wait_recv()
        if ch in CROSS_FIRST:
            core_own[ch] += core_in[ch].astype(jnp.float32)
        else:
            out = core_own[ch, 1 - x] + core_in[ch, 1 - x].astype(jnp.float32)
            x_out[ch] = out.astype(jnp.bfloat16)
            launch(functools.partial(rx, ch))
            x_own[ch] = core_own[ch, x] + core_in[ch, x].astype(jnp.float32)

    def mine(ch, index):
        if ch in CROSS_FIRST:
            return core_own.at[ch, :, block(index)]
        return x_own.at[ch, block(index)]

    def slot(ref, ch, s, g):
        return ref.at[ch, s, g] if ch in CROSS_FIRST else ref.at[ch, s, g, 0]

    def rz(ch, s, g):
        return remote(
            slot(z_out, ch, s, g), slot(z_in, ch, s, g - 1),
            rz_s.at[ch, s, g], rz_r.at[ch, s, g - 1], z_peer(s),
        )

    def rz_arrival(ch, s, g):
        ref = slot(z_in, ch, s, g)
        return remote(ref, ref, rz_s.at[ch, s, g], rz_r.at[ch, s, g], x_peer)

    def scatter_c(ch, g):
        if ch not in CROSS_FIRST and g == end:
            rx(ch).wait_recv()
            x_own[ch] += x_in[ch].astype(jnp.float32)
        for s in range(2):
            valid = z + g <= end if s == 0 else z >= g
            before = has_low if s == 0 else has_high

            def plain(g=g, s=s):
                out = mine(ch, z + signs[s] * g)[...]
                slot(z_out, ch, s, g)[...] = out.astype(jnp.bfloat16)

            def added(g=g, s=s):
                rz_arrival(ch, s, g).wait_recv()
                out = mine(ch, z + signs[s] * g)[...]
                out += slot(z_in, ch, s, g)[...].astype(jnp.float32)
                slot(z_out, ch, s, g)[...] = out.astype(jnp.bfloat16)

            pl.when(valid & jnp.logical_not(before))(plain)
            if g < end:
                pl.when(valid & before)(added)
            launch(functools.partial(rz, ch, s, g), valid)

    def scatter_d(ch):
        def add_in(s):
            rz_arrival(ch, s, 0).wait_recv()
            mine(ch, z)[...] += slot(z_in, ch, s, 0)[...].astype(jnp.float32)

        pl.when(has_low)(lambda: add_in(0))
        pl.when(has_high)(lambda: add_in(1))
        cols = slice(ch * size, (ch + 1) * size)
        if ch in CROSS_FIRST:
            at = CROSS_FIRST.index(ch)
            last_out[at] = core_own[ch, 1 - x, block(z), :].astype(jnp.bfloat16)
            launch(functools.partial(rx, ch))
        else:
            out_ref[:, cols] = x_own[ch, block(z), :].astype(jnp.bfloat16)

    def scatter_e(ch):
        at = CROSS_FIRST.index(ch)
        rx(ch).wait_recv()
        out = core_own[ch, x, block(z), :] + last_in[at].astype(jnp.float32)
        out_ref[:, ch * size : (ch + 1) * size] = out.astype(jnp.bfloat16)

    order = list(CROSS_FIRST) + [ch for ch in range(NUM_CHUNKS) if ch not in CROSS_FIRST]
    for i in range(NUM_CHUNKS + 1):
        if i < NUM_CHUNKS:
            scatter_a(order[i])
        if 0 <= i - 1:
            scatter_b(order[i - 1])
    for i in range(NUM_CHUNKS + end):
        for k in range(end):
            if 0 <= i - k < NUM_CHUNKS:
                scatter_c(order[i - k], end - k)
        if 0 <= i - end:
            scatter_d(order[i - end])
    for ch in CROSS_FIRST:
        scatter_e(ch)
    for finish in sends:
        finish()


def dense_body(tokens, route_copy, gate_value, w_gate_up, w_down):
    num_steps, tok_rows, dim = tokens.shape
    rows = num_steps * tok_rows
    wide_count = lax.axis_size("wide")
    width = w_down.shape[1]
    size = dim // NUM_CHUNKS
    col = wide_count * rows
    bf16, f32 = jnp.bfloat16, jnp.float32
    vmem = pl.BlockSpec(memory_space=pltpu.VMEM)
    hbm = pl.BlockSpec(memory_space=pl.ANY)
    dma = pltpu.SemaphoreType.DMA
    n = NUM_CHUNKS
    out = pl.pallas_call(
        functools.partial(dense_kernel, wide_count),
        out_shape=jax.ShapeDtypeStruct((rows, dim), bf16),
        in_specs=[vmem, vmem, vmem, hbm, hbm],
        out_specs=vmem,
        scratch_shapes=[
            pltpu.VMEM((2, 2, col, LANES + dim), bf16),
            pltpu.VMEM((dim, 2 * width), bf16),
            pltpu.VMEM((width, dim), bf16),
            pltpu.VMEM((4 * col, 2 * width), f32),
            pltpu.VMEM((2, 2, col, width), bf16),
            pltpu.VMEM((n, 2, col, size), bf16),
            pltpu.VMEM((n, 2, col, size), bf16),
            pltpu.VMEM((n, 2, col, size), f32),
            pltpu.VMEM((n, col, size), bf16),
            pltpu.VMEM((n, col, size), bf16),
            pltpu.VMEM((n, col, size), f32),
            pltpu.VMEM((n, 2, wide_count, 2, rows, size), bf16),
            pltpu.VMEM((n, 2, wide_count, 2, rows, size), bf16),
            pltpu.VMEM((max(1, len(CROSS_FIRST)), rows, size), bf16),
            pltpu.VMEM((max(1, len(CROSS_FIRST)), rows, size), bf16),
            dma((n,)), dma,
            dma((n, 2, wide_count)), dma((n, 2, wide_count)),
            dma((n, 3, wide_count)), dma((n, 3, wide_count)),
            dma((n,)), dma((n,)), dma((n,)), dma((n,)),
            dma((n,)), dma((n,)), dma((n,)), dma((n,)),
            dma((n, 2, wide_count)), dma((n, 2, wide_count)),
        ],
        compiler_params=pltpu.CompilerParams(
            collective_id=0, has_side_effects=True, vmem_limit_bytes=56 * 1024 * 1024
        ),
        cost_estimate=pl.CostEstimate(
            flops=12 * col * dim * width * 2, bytes_accessed=3 * dim * width * 2, transcendentals=0
        ),
    )(
        tokens.reshape(rows, dim),
        route_copy.transpose(0, 2, 1),
        gate_value.transpose(0, 2, 1),
        w_gate_up[0],
        w_down[0],
    )
    return out.reshape(num_steps, tok_rows, dim)


def choose_body(tokens, route_copy, gate_value, w_gate_up, w_down):
    wide_count = lax.axis_size("wide")
    narrow_count = lax.axis_size("narrow")
    copy_count = wide_count * narrow_count // SPLIT
    every_copy = route_copy.shape[2] == copy_count and copy_count <= THIRD
    whole_rows = tokens.shape[0] * tokens.shape[1] % 16 == 0
    if every_copy and whole_rows and narrow_count == SPLIT:
        return dense_body(tokens, route_copy, gate_value, w_gate_up, w_down)
    return body(tokens, route_copy, gate_value, w_gate_up, w_down)


def solution(mesh):
    return jax.shard_map(
        choose_body,
        mesh=mesh,
        in_specs=(
            P(None, ("parts", "wide", "narrow"), None),
            P(None, ("parts", "wide", "narrow"), None),
            P(None, ("parts", "wide", "narrow"), None),
            P(("wide", "narrow"), None, None),
            P(("wide", "narrow"), None, None),
        ),
        out_specs=P(None, ("parts", "wide", "narrow"), None),
        check_vma=False,
    )
```

```python
import functools

import jax
import jax.numpy as jnp
from jax import lax
from jax.experimental import pallas as pl
from jax.experimental.pallas import tpu as pltpu
from jax.sharding import PartitionSpec as P

SPLIT = 4


def from_partner(block, axis, bit):
    count = lax.axis_size(axis)
    route = []
    for low in range(count):
        high = low | 1 << bit
        if high != low and high < count:
            route += [(low, high), (high, low)]
    return lax.ppermute(block, axis, route)


def expert_block(packet, gate_up, down):
    width = down.shape[0]
    lead = packet.shape[:-1]
    row_block = packet.reshape(-1, packet.shape[-1])
    joined = jnp.dot(row_block, gate_up, preferred_element_type=jnp.float32)
    hidden = (jax.nn.silu(joined[:, :width]) * joined[:, width:]).astype(jnp.bfloat16)
    produced = jnp.dot(hidden, down, preferred_element_type=jnp.float32).astype(jnp.bfloat16)
    return produced.reshape(lead + (down.shape[1],))


def rank_pairs(route_now, copy_count):
    one_hot = (route_now[..., None] == jnp.arange(copy_count, dtype=jnp.int32)).astype(jnp.int32)
    counts = jnp.sum(one_hot, axis=-2)
    before = jnp.cumsum(counts, axis=-2) - counts
    return jnp.sum(one_hot * before[..., None, :], axis=-1)


def select_rows(target, gates, slot_total):
    matches = target[None, :, :] == jnp.arange(slot_total, dtype=jnp.int32)[:, None, None]
    picker = jnp.any(matches, axis=-1).astype(jnp.bfloat16)
    weights = jnp.sum(jnp.where(matches, gates[None, :, :], 0.0), axis=-1)
    return (picker, weights)


def body(tokens, route_copy, gate_value, w_gate_up, w_down):
    num_steps, tok_rows, model_dim = tokens.shape
    top_count = route_copy.shape[2]
    wide_count = lax.axis_size("wide")
    narrow_count = lax.axis_size("narrow")
    dev_count = wide_count * narrow_count
    copy_count = dev_count // SPLIT
    slot_cap = min(tok_rows, max(2, 3 * tok_rows * top_count // (2 * copy_count) + tok_rows // 64))
    gate_up = w_gate_up[0]
    down = w_down[0]
    results = []
    for step_index in range(num_steps):
        step_rows = tokens[step_index]
        step_route = route_copy[step_index]
        step_gate = gate_value[step_index]
        piece_rows = (slot_cap + SPLIT - 1) // SPLIT
        per_copy = SPLIT * piece_rows
        ranked = rank_pairs(step_route, copy_count)
        target = step_route * per_copy + ranked
        picker, weights = select_rows(target, step_gate, copy_count * per_copy)
        outbox = jnp.dot(picker, step_rows, preferred_element_type=jnp.float32).astype(jnp.bfloat16)
        outbox = outbox.reshape(dev_count, piece_rows, model_dim)
        received = lax.all_to_all(
            outbox, ("wide", "narrow"), split_axis=0, concat_axis=0, tiled=True
        )
        narrow_index = lax.axis_index("narrow")
        shared = received
        for bit_number in range(SPLIT.bit_length() - 1):
            other = from_partner(shared, "narrow", bit_number)
            upper = narrow_index >> bit_number & 1 == 1
            shared = jnp.where(
                upper,
                jnp.concatenate([other, shared], axis=1),
                jnp.concatenate([shared, other], axis=1),
            )
        produced = expert_block(shared[:, :slot_cap], gate_up, down)
        returned = lax.all_to_all(
            produced, ("wide", "narrow"), split_axis=0, concat_axis=0, tiled=True
        )
        summed = jnp.sum(
            returned.reshape(copy_count, SPLIT, slot_cap, model_dim).astype(jnp.float32), axis=1
        )
        used = weights.reshape(copy_count, per_copy, tok_rows)[:, :slot_cap].reshape(
            copy_count * slot_cap, tok_rows
        )
        total = jnp.dot(
            used.T,
            summed.reshape(copy_count * slot_cap, model_dim),
            precision=lax.Precision.HIGHEST,
        )
        results.append(total.astype(jnp.bfloat16))
    return jnp.stack(results)


UNITS = (6, 9, 6, 7)
CROSS_FIRST = (3,)
DIRECT = (0, 1, 2)
GATHER_ORDER = (0, 1, 2, 3)
SCATTER_ORDER = (3, 0, 1, 2)
NUM_CHUNKS = len(UNITS)
LANES = 128
THIRD = 32
MESH = pl.DeviceIdType.MESH


def dense_kernel(
    wide_count, tok_ref, route_ref, gate_ref, up_hbm, down_hbm, out_ref,
    held, up, down, acc, hid, core_out, core_in, core_own, x_out, x_in, x_own, z_out, z_in,
    last_out, last_in,
    up_sem, down_sem, gz_s, gz_r, gx_s, gx_r, ga_s, ga_r, gb_s, gb_r,
    rc_s, rc_r, rx_s, rx_r, rz_s, rz_r,
):
    rows, dim = tok_ref.shape
    num_steps, top_count, tok_rows = route_ref.shape
    width = down.shape[0]
    unit = dim // sum(UNITS)
    sizes = [count * unit for count in UNITS]
    starts = [sum(sizes[:ch]) for ch in range(NUM_CHUNKS)]
    part = lax.axis_index("parts")
    z = lax.axis_index("wide")
    narrow = lax.axis_index("narrow")
    x = narrow // 2
    c = narrow % 2
    x_peer = (part, z, (1 - x) * 2 + c)
    c_peer = (part, z, x * 2 + 1 - c)
    end = wide_count - 1
    has_low, has_high = z > 0, z < end
    signs = (1, -1)
    steps = [(h, s) for h in range(end) for s in range(2)]

    def block(index):
        return pl.ds(pl.multiple_of(index * rows, rows), rows)

    def cols_of(ch):
        if ch == 0:
            return pl.ds(0, LANES + sizes[0])
        return pl.ds(LANES + starts[ch], sizes[ch])

    def span_of(ch):
        return pl.ds(starts[ch], sizes[ch])

    def z_peer(s):
        return (part, z + signs[s], narrow)

    up_copies = {}
    for ch in GATHER_ORDER:
        span = span_of(ch)
        copy = pltpu.make_async_copy(up_hbm.at[span], up.at[span], up_sem.at[ch])
        copy.start()
        up_copies[ch] = copy
    down_copy = pltpu.make_async_copy(down_hbm, down, down_sem)
    down_copy.start()

    barrier = pltpu.get_barrier_semaphore()

    def greet(peer):
        pl.semaphore_signal(barrier, inc=1, device_id=peer, device_id_type=MESH)

    for k in range(1, wide_count):
        greet((part, lax.rem(z + k, wide_count), narrow))
    greet(x_peer)
    greet(c_peer)

    eye = lax.broadcasted_iota(jnp.int32, (tok_rows, tok_rows), 0) == lax.broadcasted_iota(
        jnp.int32, (tok_rows, tok_rows), 1
    )
    lane = lax.broadcasted_iota(jnp.int32, (tok_rows, LANES), 1)
    coded_steps = []
    for step in range(num_steps):
        weight = jnp.zeros((tok_rows, LANES), jnp.float32)
        for k in range(top_count):
            route = jnp.where(eye, route_ref[step, k : k + 1, :], 0)
            route = jnp.sum(route, axis=1, keepdims=True)
            gate = jnp.where(eye, gate_ref[step, k : k + 1, :], 0.0)
            gate = jnp.sum(gate, axis=1, keepdims=True)
            weight += jnp.where(lane % THIRD == route, gate, 0.0)
        high = weight.astype(jnp.bfloat16).astype(jnp.float32)
        mid = (weight - high).astype(jnp.bfloat16).astype(jnp.float32)
        low = weight - high - mid
        low = jnp.where(lane < 3 * THIRD, low, 0.0)
        coded_steps.append(jnp.where(lane < THIRD, high, jnp.where(lane < 2 * THIRD, mid, low)))
    coded = jnp.concatenate(coded_steps, axis=0).astype(jnp.bfloat16)
    held[x, c, block(z), 0:LANES] = coded
    held[x, c, block(z), LANES:] = tok_ref[...]

    pl.semaphore_wait(barrier, wide_count + 1)

    sends = []

    def remote(src, dst, send_sem, recv_sem, peer):
        return pltpu.make_async_remote_copy(
            src_ref=src, dst_ref=dst, send_sem=send_sem, recv_sem=recv_sem,
            device_id=peer, device_id_type=MESH,
        )

    def launch(make, *cond):
        def go():
            make().start()

        def finish():
            make().wait_send()

        if cond:
            pl.when(cond[0])(go)
            sends.append(lambda: pl.when(cond[0])(finish))
        else:
            go()
            sends.append(finish)

    def flush(count):
        for finish in sends[:count]:
            finish()
        del sends[:count]

    def can_recv(h, s):
        return z >= h + 1 if s == 0 else z + h + 1 <= end

    def can_send(h, s):
        return (z >= h) & has_high if s == 0 else (z + h <= end) & has_low

    def z_ref(ch, index):
        if ch in CROSS_FIRST:
            return held.at[:, c, block(index), cols_of(ch)]
        return held.at[x, c, block(index), cols_of(ch)]

    def stream(ch, h, s):
        ref = z_ref(ch, z - signs[s] * h)
        return remote(ref, ref, gz_s.at[ch, s, h], gz_r.at[ch, s, h], z_peer(s))

    def arrival(ch, h, s):
        ref = z_ref(ch, z - signs[s] * (h + 1))
        return remote(ref, ref, gz_s.at[ch, s, h], gz_r.at[ch, s, h], x_peer)

    def own_x(ch):
        ref = held.at[x, c, block(z), cols_of(ch)]
        return remote(ref, ref, gx_s.at[ch, 2, 0], gx_r.at[ch, 2, 0], x_peer)

    def forward_x(ch, h, s):
        ref = held.at[x, c, block(z - signs[s] * (h + 1)), cols_of(ch)]
        return remote(ref, ref, gx_s.at[ch, s, h], gx_r.at[ch, s, h], x_peer)

    def core_a(ch):
        if ch in CROSS_FIRST:
            ref = held.at[:, c, :, cols_of(ch)]
        else:
            ref = held.at[x, c, :, cols_of(ch)]
        return remote(ref, ref, ga_s.at[ch], ga_r.at[ch], c_peer)

    def core_b(ch):
        ref = held.at[1 - x, c, :, cols_of(ch)]
        return remote(ref, ref, gb_s.at[ch], gb_r.at[ch], c_peer)

    for ch in GATHER_ORDER:
        if ch not in CROSS_FIRST:
            for s in range(2):
                launch(functools.partial(stream, ch, 0, s), can_send(0, s))
        launch(functools.partial(own_x, ch))

    def gather_first(ch):
        if ch in CROSS_FIRST:
            own_x(ch).wait_recv()
            for s in range(2):
                launch(functools.partial(stream, ch, 0, s), can_send(0, s))

    def gather_a(ch, h):
        for s in range(2):
            pl.when(can_recv(h, s))(lambda h=h, s=s: arrival(ch, h, s).wait_recv())
            if h + 1 < end:
                launch(functools.partial(stream, ch, h + 1, s), can_send(h + 1, s))
            if ch not in CROSS_FIRST:
                launch(functools.partial(forward_x, ch, h, s), can_recv(h, s))
        if h + 1 == end:
            launch(functools.partial(core_a, ch))

    def gather_b(ch):
        if ch not in CROSS_FIRST:
            own_x(ch).wait_recv()
            for h, s in steps:
                pl.when(can_recv(h, s))(lambda h=h, s=s: forward_x(ch, h, s).wait_recv())
            launch(functools.partial(core_b, ch))

    def gather_c(ch):
        core_a(ch).wait_recv()
        if ch not in CROSS_FIRST:
            core_b(ch).wait_recv()
        up_copies[ch].wait()
        cols = held[:, :, :, pl.ds(LANES + starts[ch], sizes[ch])]
        term = jnp.dot(
            cols.reshape(-1, sizes[ch]), up[span_of(ch), :],
            preferred_element_type=jnp.float32,
        )
        if ch == GATHER_ORDER[0]:
            acc[...] = term
        else:
            acc[...] += term

    for i in range(NUM_CHUNKS + end + 1):
        if i < NUM_CHUNKS:
            gather_first(GATHER_ORDER[i])
        for h in range(end):
            if 0 <= i - h < NUM_CHUNKS:
                gather_a(GATHER_ORDER[i - h], h)
        if 0 <= i - end < NUM_CHUNKS:
            gather_b(GATHER_ORDER[i - end])
        if 0 <= i - end - 1:
            gather_c(GATHER_ORDER[i - end - 1])

    gathered = len(sends)
    joined = acc[...]
    gate = joined[:, :width]
    value = gate / (1.0 + jnp.exp(-gate)) * joined[:, width:]
    hid[...] = value.astype(jnp.bfloat16).reshape(hid.shape)
    down_copy.wait()

    def row_weights(core):
        coded = held[:, core, :, 0:LANES].reshape(-1, LANES).astype(jnp.float32)
        lane = lax.broadcasted_iota(jnp.int32, coded.shape, 1)
        return jnp.sum(jnp.where(lane % THIRD == z, coded, 0.0), axis=1, keepdims=True)

    other_weight = row_weights(1 - c)
    own_weight = row_weights(c)
    col = wide_count * rows

    def rc(ch):
        return remote(core_out.at[:, :, span_of(ch)], core_in.at[:, :, span_of(ch)], rc_s.at[ch], rc_r.at[ch], c_peer)

    def rx(ch):
        if ch in CROSS_FIRST:
            return remote(last_out.at[:, span_of(ch)], last_in.at[:, span_of(ch)], rx_s.at[ch], rx_r.at[ch], x_peer)
        return remote(x_out.at[:, span_of(ch)], x_in.at[:, span_of(ch)], rx_s.at[ch], rx_r.at[ch], x_peer)

    def scatter_a(ch):
        cols = span_of(ch)
        half = (2, col, sizes[ch])
        out = jnp.dot(
            hid[:, 1 - c].reshape(-1, width), down[:, cols], preferred_element_type=jnp.float32
        )
        core_out[:, :, cols] = (out * other_weight).astype(jnp.bfloat16).reshape(half)
        launch(functools.partial(rc, ch))
        out = jnp.dot(
            hid[:, c].reshape(-1, width), down[:, cols], preferred_element_type=jnp.float32
        )
        core_own[:, :, cols] = (out * own_weight).reshape(half)

    def scatter_b(ch):
        rc(ch).wait_recv()
        cols = span_of(ch)
        if ch in CROSS_FIRST:
            core_own[:, :, cols] += core_in[:, :, cols].astype(jnp.float32)
        else:
            out = core_own[1 - x, :, cols] + core_in[1 - x, :, cols].astype(jnp.float32)
            x_out[:, cols] = out.astype(jnp.bfloat16)
            launch(functools.partial(rx, ch))
            x_own[:, cols] = core_own[x, :, cols] + core_in[x, :, cols].astype(jnp.float32)

    def mine(ch, index):
        if ch in CROSS_FIRST:
            return core_own.at[:, block(index), span_of(ch)]
        return x_own.at[block(index), span_of(ch)]

    def slot(ref, ch, s, g):
        if ch in CROSS_FIRST:
            return ref.at[s, g, :, :, span_of(ch)]
        return ref.at[s, g, 0, :, span_of(ch)]

    def rz(ch, s, g):
        return remote(
            slot(z_out, ch, s, g), slot(z_in, ch, s, g - 1),
            rz_s.at[ch, s, g], rz_r.at[ch, s, g - 1], z_peer(s),
        )

    def rz_direct(ch, s, g):
        return remote(
            slot(z_out, ch, s, g), slot(z_in, ch, s, g - 1),
            rz_s.at[ch, s, g], rz_r.at[ch, s, g - 1], (part, z + signs[s] * g, narrow),
        )

    def send_direct(ch):
        for g in range(1, wide_count):
            for s in range(2):
                valid = z + g <= end if s == 0 else z >= g

                def fill(g=g, s=s):
                    out = mine(ch, z + signs[s] * g)[...]
                    slot(z_out, ch, s, g)[...] = out.astype(jnp.bfloat16)

                pl.when(valid)(fill)
                launch(functools.partial(rz_direct, ch, s, g), valid)

    def rz_arrival(ch, s, g):
        ref = slot(z_in, ch, s, g)
        return remote(ref, ref, rz_s.at[ch, s, g], rz_r.at[ch, s, g], x_peer)

    def scatter_c(ch, g):
        if ch not in CROSS_FIRST and g == end:
            rx(ch).wait_recv()
            x_own[:, span_of(ch)] += x_in[:, span_of(ch)].astype(jnp.float32)
        if ch in DIRECT:
            if g == end:
                send_direct(ch)
            return
        for s in range(2):
            valid = z + g <= end if s == 0 else z >= g
            before = has_low if s == 0 else has_high

            def plain(g=g, s=s):
                out = mine(ch, z + signs[s] * g)[...]
                slot(z_out, ch, s, g)[...] = out.astype(jnp.bfloat16)

            def added(g=g, s=s):
                rz_arrival(ch, s, g).wait_recv()
                out = mine(ch, z + signs[s] * g)[...]
                out += slot(z_in, ch, s, g)[...].astype(jnp.float32)
                slot(z_out, ch, s, g)[...] = out.astype(jnp.bfloat16)

            pl.when(valid & jnp.logical_not(before))(plain)
            if g < end:
                pl.when(valid & before)(added)
            launch(functools.partial(rz, ch, s, g), valid)

    def scatter_d(ch):
        def add_in(s, g):
            rz_arrival(ch, s, g).wait_recv()
            mine(ch, z)[...] += slot(z_in, ch, s, g)[...].astype(jnp.float32)

        for g in range(end if ch in DIRECT else 1):
            pl.when(z > g)(lambda g=g: add_in(0, g))
            pl.when(z + g < end)(lambda g=g: add_in(1, g))
        cols = span_of(ch)
        if ch in CROSS_FIRST:
            last_out[:, cols] = core_own[1 - x, block(z), cols].astype(jnp.bfloat16)
            launch(functools.partial(rx, ch))
        else:
            out_ref[:, cols] = x_own[block(z), cols].astype(jnp.bfloat16)

    def scatter_e(ch):
        rx(ch).wait_recv()
        cols = span_of(ch)
        out = core_own[x, block(z), cols] + last_in[:, cols].astype(jnp.float32)
        out_ref[:, cols] = out.astype(jnp.bfloat16)

    order = SCATTER_ORDER
    for i in range(NUM_CHUNKS + 1):
        if i < NUM_CHUNKS:
            scatter_a(order[i])
        if 0 <= i - 1:
            scatter_b(order[i - 1])
    flush(gathered)
    for i in range(NUM_CHUNKS + end):
        if i + 1 == NUM_CHUNKS + end:
            flush(len(sends) - 2 * end)
        for k in range(end):
            if 0 <= i - k < NUM_CHUNKS:
                scatter_c(order[i - k], end - k)
        if 0 <= i - end:
            scatter_d(order[i - end])
    for ch in CROSS_FIRST:
        scatter_e(ch)
    flush(len(sends))


def dense_body(tokens, route_copy, gate_value, w_gate_up, w_down):
    num_steps, tok_rows, dim = tokens.shape
    rows = num_steps * tok_rows
    wide_count = lax.axis_size("wide")
    width = w_down.shape[1]
    col = wide_count * rows
    bf16, f32 = jnp.bfloat16, jnp.float32
    vmem = pl.BlockSpec(memory_space=pltpu.VMEM)
    hbm = pl.BlockSpec(memory_space=pl.ANY)
    dma = pltpu.SemaphoreType.DMA
    n = NUM_CHUNKS
    out = pl.pallas_call(
        functools.partial(dense_kernel, wide_count),
        out_shape=jax.ShapeDtypeStruct((rows, dim), bf16),
        in_specs=[vmem, vmem, vmem, hbm, hbm],
        out_specs=vmem,
        scratch_shapes=[
            pltpu.VMEM((2, 2, col, LANES + dim), bf16),
            pltpu.VMEM((dim, 2 * width), bf16),
            pltpu.VMEM((width, dim), bf16),
            pltpu.VMEM((4 * col, 2 * width), f32),
            pltpu.VMEM((2, 2, col, width), bf16),
            pltpu.VMEM((2, col, dim), bf16),
            pltpu.VMEM((2, col, dim), bf16),
            pltpu.VMEM((2, col, dim), f32),
            pltpu.VMEM((col, dim), bf16),
            pltpu.VMEM((col, dim), bf16),
            pltpu.VMEM((col, dim), f32),
            pltpu.VMEM((2, wide_count, 2, rows, dim), bf16),
            pltpu.VMEM((2, wide_count, 2, rows, dim), bf16),
            pltpu.VMEM((rows, dim), bf16),
            pltpu.VMEM((rows, dim), bf16),
            dma((n,)), dma,
            dma((n, 2, wide_count)), dma((n, 2, wide_count)),
            dma((n, 3, wide_count)), dma((n, 3, wide_count)),
            dma((n,)), dma((n,)), dma((n,)), dma((n,)),
            dma((n,)), dma((n,)), dma((n,)), dma((n,)),
            dma((n, 2, wide_count)), dma((n, 2, wide_count)),
        ],
        compiler_params=pltpu.CompilerParams(
            collective_id=0, has_side_effects=True, vmem_limit_bytes=56 * 1024 * 1024
        ),
        cost_estimate=pl.CostEstimate(
            flops=12 * col * dim * width * 2, bytes_accessed=3 * dim * width * 2, transcendentals=0
        ),
    )(
        tokens.reshape(rows, dim),
        route_copy.transpose(0, 2, 1),
        gate_value.transpose(0, 2, 1),
        w_gate_up[0],
        w_down[0],
    )
    return out.reshape(num_steps, tok_rows, dim)


def choose_body(tokens, route_copy, gate_value, w_gate_up, w_down):
    wide_count = lax.axis_size("wide")
    narrow_count = lax.axis_size("narrow")
    copy_count = wide_count * narrow_count // SPLIT
    every_copy = route_copy.shape[2] == copy_count and copy_count <= THIRD
    whole_rows = tokens.shape[0] * tokens.shape[1] % 16 == 0
    whole_units = tokens.shape[2] % (sum(UNITS) * 128) == 0
    if every_copy and whole_rows and whole_units and narrow_count == SPLIT:
        return dense_body(tokens, route_copy, gate_value, w_gate_up, w_down)
    return body(tokens, route_copy, gate_value, w_gate_up, w_down)


def solution(mesh):
    return jax.shard_map(
        choose_body,
        mesh=mesh,
        in_specs=(
            P(None, ("parts", "wide", "narrow"), None),
            P(None, ("parts", "wide", "narrow"), None),
            P(None, ("parts", "wide", "narrow"), None),
            P(("wide", "narrow"), None, None),
            P(("wide", "narrow"), None, None),
        ),
        out_specs=P(None, ("parts", "wide", "narrow"), None),
        check_vma=False,
    )
```
